32 devices in a mesh: runs: 2 (over y), tiles: 4 (over z), bands: 4 (over x, core).
Axes of the slice: x: 2, y: 2, z: 4, core: 2. Of those that a mesh axis runs over, the one named last changes fastest.
Arguments:
- spectra: float32 [48, 36, 128, 128], P('bands', None, ('runs', 'tiles')), parts along dimension 2, may hold values from 0.05 to 2
- sea_mask: int32 [128, 128], P('runs'), parts along dimension 0, may hold values from 0 to 1, as said below
- neighbors: int32 [4, 128, 128], P(None, ('runs', 'tiles')), parts along dimension 1, may hold values from 0 to 2304, as said below
- courant: float32 [128, 128], P(('runs', 'tiles')), parts along dimension 0, may hold values from 0.2 to 0.7
- turning: float32 [128, 128], P(('runs', 'tiles')), parts along dimension 0, may hold values from -0.3 to 0.3
- wind_speed: float32 [128, 128], P(('runs', 'tiles')), parts along dimension 0, may hold values from 0.2 to 1
- wind_dir: float32 [128, 128], P(('runs', 'tiles')), parts along dimension 0, may hold values from -3.140625 to 3.140625
Outputs:
- new_spectra: float32 [48, 36, 128, 128], P('bands', None, ('runs', 'tiles')), parts along dimension 2
The draws below stay inside these ranges and needn't reach their ends.
There are 2 independent parts, one for each index of `runs`. The reference program is written for one: setup_inputs(seed, part) draws one part's arguments, and reference() takes and returns one part's arrays. A program takes and returns all parts, laid end to end along the dimension named above; each array names one. Nothing has to cross between parts.
Inputs may be any that keep to these rules, and one draw needn't show every extreme that they name: `sea_mask`: exactly 32 tiles hold one or more sea points, among them the first and the last tile of every block of 16 tiles; every point of the other tiles is land. neighbors[k, t, p] names the west (k = 0), east (1), south (2) and north (3) neighbour of point p of tile t as (tile - first tile of t's block of 16 tiles + 1) * 128 + point, where west and east lie in tile t, south in tile t - 1 and north in tile t + 1; (18) * 128 means no neighbour.
All inputs are finite; a program needn't handle non-finite values.
Results may differ from the reference program's by a relative error of at most 0.0003.
Values sent between devices are 32-bit elements; how exact they have to be, the bound alone decides.
A program may use at most 64 MiB of HBM per device.

```python
import math
import jax
import jax.numpy as jnp
from jax import lax

NF = 48
ND = 36
TP = 128
TILE_DEV = 16
NTILES = 64


def draw_sea_mask(key, part):
    key = jax.random.fold_in(key, 11)
    sub_keys = jax.random.split(key, 4)
    cluster = jax.random.randint(sub_keys[0], (NTILES // TILE_DEV,), 0, 4)
    tile_order = jax.random.permutation(sub_keys[1], NTILES)
    local_tile = jnp.arange(NTILES) % TILE_DEV
    edge_tile = ((local_tile == 0) | (local_tile == TILE_DEV - 1)).astype(jnp.int32)
    tile_score = edge_tile * (5 * NTILES) + jnp.repeat(cluster, TILE_DEV) * NTILES + tile_order
    top_scores, wet_ids = lax.top_k(tile_score, NTILES // 2)
    wet_tile = jnp.zeros((NTILES,), jnp.int32).at[wet_ids].set(1)
    sea_point = jax.random.randint(sub_keys[2], (NTILES, TP), 0, 5) > 0
    keeper = jax.random.randint(sub_keys[3], (NTILES, 1), 0, TP)
    sea_point = sea_point | (jnp.arange(TP)[None, :] == keeper)
    return (sea_point & (wet_tile[:, None] > 0)).astype(jnp.int32)


def draw_neighbors(key, part):
    key = jax.random.fold_in(key, 23)
    tile_keys = jax.random.split(key, NTILES)
    column = jax.vmap(lambda single: jax.random.permutation(single, TP))(tile_keys)
    inverse = jnp.argsort(column, axis=1).astype(jnp.int32)
    land_index = (TILE_DEV + 2) * TP
    local_tile = jnp.arange(NTILES) % TILE_DEV
    own_base = ((local_tile + 1) * TP)[:, None]
    west_link = jnp.where(column > 0, own_base + jnp.take_along_axis(inverse, jnp.maximum(column - 1, 0), axis=1), land_index)
    east_link = jnp.where(column < TP - 1, own_base + jnp.take_along_axis(inverse, jnp.minimum(column + 1, TP - 1), axis=1), land_index)
    south_link = (local_tile * TP)[:, None] + jnp.take_along_axis(jnp.roll(inverse, 1, axis=0), column, axis=1)
    north_link = ((local_tile + 2) * TP)[:, None] + jnp.take_along_axis(jnp.roll(inverse, -1, axis=0), column, axis=1)
    return jnp.stack([west_link, east_link, south_link, north_link]).astype(jnp.int32)


def steps_of(own_key, dims, pieces, low, top_value):
    loudness = 1.0
    for dim, shards_of in pieces:
        draws = jax.random.uniform(jax.random.fold_in(jax.random.fold_in(own_key, 6), dim), (shards_of,), jnp.float32, low / len(pieces), top_value / len(pieces))
        loudness = loudness * jnp.repeat(jnp.exp(draws), dims[dim] // shards_of).reshape((-1,) + (1,) * (len(dims) - 1 - dim))
    return loudness


def setup_inputs(seed: int = 0, part: int = 0) -> dict:
    key_list = jax.random.split(jax.random.key(seed), 8)
    part_splits = jax.random.split(jax.random.fold_in(key_list[7], part), 8)
    return {
        "spectra": jnp.clip(jnp.exp(math.log(2.0) - 3.6888794 * jax.random.uniform(part_splits[0], (NF, ND, NTILES, TP), jnp.float32) ** steps_of(part_splits[0], (NF, ND, NTILES, TP), ((0, 4), (2, 4)), -0.2, 0.2)), 0.05, 2.0),
        "sea_mask": draw_sea_mask(jax.random.fold_in(jax.random.fold_in(key_list[7], part), 71), part),
        "neighbors": draw_neighbors(jax.random.fold_in(jax.random.fold_in(key_list[7], part), 71), part),
        "courant": jnp.clip(0.2 + 0.5 * jax.random.uniform(part_splits[3], (NTILES, TP), jnp.float32) ** steps_of(part_splits[3], (NTILES, TP), ((0, 4),), -0.2, 0.2), 0.2, 0.7),
        "turning": jnp.clip(jax.random.uniform(part_splits[4], (NTILES, TP), jnp.float32, -0.3, 0.3) * steps_of(part_splits[4], (NTILES, TP), ((0, 4),), -0.4, 0.0), -0.3, 0.3),
        "wind_speed": jnp.clip(0.2 + 0.8 * jax.random.uniform(part_splits[5], (NTILES, TP), jnp.float32) ** steps_of(part_splits[5], (NTILES, TP), ((0, 4),), -0.2, 0.2), 0.2, 1.0),
        "wind_dir": jnp.clip(jax.random.uniform(part_splits[6], (NTILES, TP), jnp.float32, -3.140625, 3.140625), -3.140625, 3.140625),
    }


def directions_table(dir_count):
    angles = 2.0 * math.pi * (jnp.arange(dir_count).astype(jnp.float32) + 0.5) / dir_count
    return jnp.cos(angles), jnp.sin(angles)


def propagate(spectrum, extended, link_table, sea_float, courant, turning, speed_ratio, cosines, sine_table):
    band_width, dir_count, tiles_here, points = spectrum.shape
    ext_length = extended.shape[2] * points
    flattened = extended.reshape(band_width, dir_count, ext_length)
    link_flat = link_table.reshape(-1)
    in_basin = (link_flat < ext_length).astype(jnp.float32)
    beside = jnp.take(flattened, jnp.minimum(link_flat, ext_length - 1), axis=2) * in_basin
    beside = beside.reshape(band_width, dir_count, 4, tiles_here, points)
    group_speed = speed_ratio[:, None, None, None] * courant[None, None]
    along_x = group_speed * cosines[None, :, None, None]
    along_y = group_speed * sine_table[None, :, None, None]
    advected = (spectrum
                - jnp.maximum(along_x, 0.0) * (spectrum - beside[:, :, 0])
                - jnp.maximum(-along_x, 0.0) * (spectrum - beside[:, :, 1])
                - jnp.maximum(along_y, 0.0) * (spectrum - beside[:, :, 2])
                - jnp.maximum(-along_y, 0.0) * (spectrum - beside[:, :, 3]))
    advected = advected * sea_float[None, None]
    turn_rate = (0.5 + 0.5 * speed_ratio)[:, None, None, None] * turning[None, None]
    lower_dir = jnp.roll(advected, 1, axis=1)
    upper_dir = jnp.roll(advected, -1, axis=1)
    return (advected - jnp.maximum(turn_rate, 0.0) * (advected - lower_dir)
            - jnp.maximum(-turn_rate, 0.0) * (advected - upper_dir))


def sources(spectrum, wind_east, wind_north):
    freq_count, dir_count = spectrum.shape[0], spectrum.shape[1]
    fraction = (jnp.arange(freq_count).astype(jnp.float32) / (freq_count - 1))[:, None, None, None]
    cosines, sine_table = directions_table(dir_count)
    steepness = jnp.sum((0.5 + fraction) * spectrum, axis=(0, 1)) / (freq_count * dir_count)
    facing = wind_east[None, None] * cosines[None, :, None, None] + wind_north[None, None] * sine_table[None, :, None, None]
    growth = 0.5 * fraction * jnp.maximum(facing, 0.0)
    damping = (0.2 + fraction) * (steepness / (steepness + 1.0))[None, None]
    widened = jnp.pad(spectrum, ((2, 2), (0, 0), (0, 0), (0, 0)))
    higher = widened[4:]
    lower_band = widened[:freq_count]
    first_up = jnp.roll(higher, -3, axis=1)
    first_down = jnp.roll(lower_band, 3, axis=1)
    second_up = jnp.roll(higher, 3, axis=1)
    second_down = jnp.roll(lower_band, -3, axis=1)
    quadruplet = (spectrum * spectrum * (first_up + first_down + second_up + second_down)
                  - 2.0 * spectrum * (first_up * first_down + second_up * second_down))
    return spectrum * jnp.exp(growth - damping) + 0.05 * (1.0 + fraction) * quadruplet


def reference(spectra, sea_mask, neighbors, courant, turning, wind_speed, wind_dir):
    sea_float = sea_mask.astype(jnp.float32)
    masked = spectra * sea_float[None, None]
    padded = jnp.pad(masked, ((0, 0), (0, 0), (1, 1), (0, 0)))
    speed_ratio = jnp.power(jnp.float32(1.1), -jnp.arange(NF).astype(jnp.float32))
    cosines, sine_table = directions_table(ND)
    wind_east = wind_speed * jnp.cos(wind_dir)
    wind_north = wind_speed * jnp.sin(wind_dir)

    def one_block(block_index):
        first_tile = block_index * TILE_DEV
        extended = lax.dynamic_slice_in_dim(padded, first_tile, TILE_DEV + 2, 2)
        own_block = lax.dynamic_slice_in_dim(masked, first_tile, TILE_DEV, 2)
        link_table = lax.dynamic_slice_in_dim(neighbors, first_tile, TILE_DEV, 1)

        def own_rows(full_table):
            return lax.dynamic_slice_in_dim(full_table, first_tile, TILE_DEV, 0)

        stepped = propagate(own_block, extended, link_table, own_rows(sea_float), own_rows(courant),
                            own_rows(turning), speed_ratio, cosines, sine_table)
        return sources(stepped, own_rows(wind_east), own_rows(wind_north))

    blocks = lax.map(one_block, jnp.arange(NTILES // TILE_DEV, dtype=jnp.int32))
    return jnp.transpose(blocks, (1, 2, 0, 3, 4)).reshape(NF, ND, NTILES, TP)
```

```python
import functools
import math

import jax
import jax.numpy as jnp
from jax import lax
from jax.experimental import pallas as pl
from jax.experimental.pallas import tpu as pltpu
from jax.sharding import PartitionSpec as P

MESH = pl.DeviceIdType.MESH
F32 = jnp.float32
LOG2E = 1.0 / math.log(2.0)
GROUP = 2


def lane_gather(x, idx):
    return jnp.take_along_axis(x, idx, axis=1, mode="promise_in_bounds")


def sin_cos(angle):
    y = 0.5 * angle
    z = y * y
    s = 1.0
    for n in (12, 10, 8, 6, 4, 2):
        s = 1.0 - z * s * (1.0 / (n * (n + 1)))
    c = 1.0
    for n in (13, 11, 9, 7, 5, 3, 1):
        c = 1.0 - z * c * (1.0 / (n * (n + 1)))
    s = s * y
    return 2.0 * s * c, 1.0 - 2.0 * s * s


def kernel(
    n_bands, n_tiles, bw, nd, tp, width,
    spectra, mask, nbr, courant, turning, wspeed, wdir, out,
    ext, e1, e2, obuf, ftab, mext, weights, lanes, hsend, hrecv, macc, mrecv,
    load_sem, out_sem, band_send, band_recv, tile_send, tile_recv,
    diag_send, diag_recv, m_send, m_recv,
):
    band = lax.axis_index("bands")
    tile = lax.axis_index("tiles")
    groups = bw // GROUP
    grows = GROUP * nd
    rows = tp + 16
    nf = n_bands * bw
    flat = ext.reshape((bw + 4) * nd * rows, width)
    has_tile = (tile > 0, tile < n_tiles - 1)
    has_band = (band > 0, band < n_bands - 1)
    step = (-1, 1)

    def load(i):
        return pltpu.make_async_copy(
            spectra.at[i], ext.at[i + 2, :, 8 : 8 + tp, :], load_sem.at[i]
        )

    for i in range(bw):
        load(i).start()

    barrier = pltpu.get_barrier_semaphore()
    for k in range(1, n_bands):
        pl.semaphore_signal(
            barrier, inc=1, device_id={"bands": lax.rem(band + k, n_bands)}, device_id_type=MESH
        )
    for dt in (1, n_tiles - 1):
        for db in (0, 1, n_bands - 1):
            pl.semaphore_signal(
                barrier, inc=1,
                device_id={
                    "bands": lax.rem(band + db, n_bands), "tiles": lax.rem(tile + dt, n_tiles)
                },
                device_id_type=MESH,
            )
    pl.semaphore_wait(barrier, n_bands - 1 + 6)

    def band_copy(side):
        first, place = (bw - 2, 0) if side == 0 else (0, bw + 2)
        return pltpu.make_async_remote_copy(
            src_ref=spectra.at[first : first + 2],
            dst_ref=ext.at[place : place + 2, :, 8 : 8 + tp, :],
            send_sem=band_send.at[side], recv_sem=band_recv.at[side],
            device_id={"bands": band - step[side]}, device_id_type=MESH,
        )

    def tile_copy(side, g):
        first = pl.multiple_of(g * grows, 8)
        return pltpu.make_async_remote_copy(
            src_ref=hsend.at[side, pl.ds(first, grows), :],
            dst_ref=hrecv.at[side, pl.ds(first + 2 * nd, grows), :],
            send_sem=tile_send.at[side, g], recv_sem=tile_recv.at[side, g],
            device_id={"tiles": tile - step[side]}, device_id_type=MESH,
        )

    def diag_copy(bside, side):
        first, place = ((bw - 2) * nd, 0) if bside == 0 else (0, (bw + 2) * nd)
        return pltpu.make_async_remote_copy(
            src_ref=hsend.at[side, pl.ds(first, 2 * nd), :],
            dst_ref=hrecv.at[side, pl.ds(place, 2 * nd), :],
            send_sem=diag_send.at[bside, side], recv_sem=diag_recv.at[bside, side],
            device_id={"bands": band - step[bside], "tiles": tile - step[side]},
            device_id_type=MESH,
        )

    def m_copy(k):
        return pltpu.make_async_remote_copy(
            src_ref=macc, dst_ref=mrecv.at[k],
            send_sem=m_send.at[k], recv_sem=m_recv.at[k],
            device_id={"bands": lax.rem(band + k, n_bands)}, device_id_type=MESH,
        )

    for side in (0, 1):
        @pl.when(has_band[1 - side])
        def _(side=side):
            band_copy(side).start()

    for g in range(groups):
        for i in range(g * GROUP, (g + 1) * GROUP):
            load(i).wait()
        base = (g * GROUP + 2) * nd * rows
        for side, row in ((0, 8 + tp - 1), (1, 8)):
            hsend[side, pl.ds(g * grows, grows), :] = flat[pl.ds(base + row, grows, stride=rows), :]
            @pl.when(has_tile[1 - side])
            def _(side=side, g=g):
                tile_copy(side, g).start()
    for side in (0, 1):
        for bside in (0, 1):
            @pl.when(has_tile[1 - side] & has_band[1 - bside])
            def _(side=side, bside=bside):
                diag_copy(bside, side).start()

    first_tile = tile * tp
    below = pl.multiple_of(jnp.maximum(first_tile - 8, 0), 8)
    above = pl.multiple_of(jnp.minimum(first_tile + tp, n_tiles * tp - 8), 8)
    mext[0:8, :] = mask[pl.ds(below, 8), :].astype(F32) * jnp.where(tile > 0, 1.0, 0.0)
    mext[8 : 8 + tp, :] = mask[pl.ds(pl.multiple_of(first_tile, 8), tp), :].astype(F32)
    mext[8 + tp :, :] = mask[pl.ds(above, 8), :].astype(F32) * jnp.where(
        tile < n_tiles - 1, 1.0, 0.0
    )
    for side in (0, 1):
        @pl.when(jnp.logical_not(has_tile[side]))
        def _(side=side):
            hrecv[side] = jnp.zeros(hrecv.shape[1:], F32)
    shifts = (0, 0, -1, 1)
    for h in range(0, tp, 8):
        here = pl.ds(h, 8)
        own = mext[8 + h : 16 + h, :]
        cm = courant[here, :] * own
        for d in range(4):
            link = nbr[d, here, :]
            lane = jnp.bitwise_and(link, width - 1)
            there = lane_gather(mext[8 + h + shifts[d] : 16 + h + shifts[d], :], lane)
            lanes[d, here, :] = lane
            weights[d, here, :] = cm * jnp.where(link < (tp + 2) * width, there, 0.0)
        weights[4, here, :] = cm
        sw, cw = sin_cos(wdir[here, :])
        east, north = wspeed[here, :] * cw, wspeed[here, :] * sw
        for j in range(nd):
            angle = 2.0 * math.pi * (j + 0.5) / nd
            facing = east * math.cos(angle) + north * math.sin(angle)
            ftab[j, here, :] = (0.5 * LOG2E) * jnp.maximum(facing, 0.0)
    macc[...] = jnp.zeros(macc.shape, F32)

    quarter = nd // 4

    def advance(e, summed):
        index = (band * bw + e - 2).astype(F32)
        fraction = index * (1.0 / (nf - 1))
        ratio = jnp.exp(jnp.full((8, width), index, F32) * (-math.log(1.1)))
        for h in range(0, tp, 8):
            here = pl.ds(h, 8)
            own = mext[8 + h : 16 + h, :]
            lane = [lanes[d, here, :] for d in range(4)]
            weight = [weights[d, here, :] * ratio for d in range(4)]
            rcm = weights[4, here, :] * ratio
            total = None
            for k in range(quarter):
                angle = 2.0 * math.pi * (k + 0.5) / nd
                c, s = math.cos(angle), math.sin(angle)
                wx = (weight[0] * c, weight[1] * c)
                wy = (weight[2] * s, weight[3] * s)
                centre = own - rcm * (c + s)
                for j, x, y in (
                    (k, 0, 0), (nd // 2 - 1 - k, 1, 0), (nd // 2 + k, 1, 1), (nd - 1 - k, 0, 1)
                ):
                    mid = ext[e, j, 8 + h : 16 + h, :]
                    off = 8 + h + (1 if y else -1)
                    beside = ext[e, j, off : off + 8, :]
                    value = (
                        centre * mid
                        + wx[x] * lane_gather(mid, lane[x])
                        + wy[y] * lane_gather(beside, lane[2 + y])
                    )
                    e1[j, here, :] = value
                    total = value if total is None else total + value
            if summed:
                macc[here, :] += (0.5 + fraction) * total
            turn = turning[here, :]
            amount = jnp.abs(turn * (0.5 + 0.5 * ratio))
            lower = turn > 0.0
            prev, now = e1[nd - 1, here, :], e1[0, here, :]
            first = now
            for j in range(nd):
                after = e1[j + 1, here, :] if j < nd - 1 else first
                e2[e, j, here, :] = now + amount * (jnp.where(lower, prev, after) - now)
                prev, now = now, after

    def fill_edges(e, count):
        first = pl.multiple_of(e * nd, 4)
        for side, row in ((0, 7), (1, 8 + tp)):
            flat[pl.ds(e * nd * rows + row, count * nd, stride=rows), :] = hrecv[
                side, pl.ds(first, count * nd), :
            ]

    def own_group(g, carry):
        for side in (0, 1):
            @pl.when(has_tile[side])
            def _(side=side):
                tile_copy(side, g).wait_recv()
        fill_edges(2 + g * GROUP, GROUP)

        def one(u, c):
            advance(2 + g * GROUP + u, True)
            return c

        return lax.fori_loop(0, GROUP, one, carry)

    lax.fori_loop(0, groups, own_group, 0)

    for k in range(1, n_bands):
        m_copy(k).start()

    for bside, place in ((0, 0), (1, bw + 2)):
        @pl.when(has_band[bside])
        def _(bside=bside, place=place):
            band_copy(bside).wait_recv()
            for side in (0, 1):
                @pl.when(has_tile[side])
                def _(side=side):
                    diag_copy(bside, side).wait_recv()
            fill_edges(place, 2)

            def one(u, c):
                advance(place + u, False)
                return c

            lax.fori_loop(0, 2, one, 0)

        @pl.when(jnp.logical_not(has_band[bside]))
        def _(place=place):
            e2[place : place + 2] = jnp.zeros((2,) + e2.shape[1:], F32)

    m_sum = macc[...]
    for k in range(1, n_bands):
        m_copy(k).wait()
        m_sum = m_sum + mrecv[k]
    m_sum = m_sum * (1.0 / (nf * nd))
    mrecv[0] = LOG2E * (m_sum / (m_sum + 1.0))

    def store(i):
        return pltpu.make_async_copy(obuf.at[i], out.at[i], out_sem.at[i])

    def finish(i, carry):
        index = (band * bw + i).astype(F32)
        fraction = index * (1.0 / (nf - 1))
        k = 0.05 * (1.0 + fraction)
        for h in range(0, tp, 8):
            here = pl.ds(h, 8)
            damping = (0.2 + fraction) * mrecv[0, here, :]
            for j in range(nd):
                up, down = (j + 3) % nd, (j - 3) % nd
                a1, a2 = e2[i + 4, up, here, :], e2[i + 4, down, here, :]
                b1, b2 = e2[i, down, here, :], e2[i, up, here, :]
                mid = e2[i + 2, j, here, :]
                gain = jnp.exp2(fraction * ftab[j, here, :] - damping)
                inner = mid * ((a1 + b1) + (a2 + b2)) - 2.0 * (a1 * b1 + a2 * b2)
                obuf[i, j, here, :] = mid * (gain + k * inner)
        store(i).start()
        return carry

    lax.fori_loop(0, bw, finish, 0)

    for i in range(bw):
        store(i).wait()
    for side in (0, 1):
        @pl.when(has_band[1 - side])
        def _(side=side):
            band_copy(side).wait_send()

        @pl.when(has_tile[1 - side])
        def _(side=side):
            for g in range(groups):
                tile_copy(side, g).wait_send()

        for bside in (0, 1):
            @pl.when(has_tile[1 - side] & has_band[1 - bside])
            def _(side=side, bside=bside):
                diag_copy(bside, side).wait_send()


def solution(mesh):
    n_bands, n_tiles = mesh.shape["bands"], mesh.shape["tiles"]

    def per_device(spectra, sea_mask, neighbors, courant, turning, wind_speed, wind_dir):
        bw, nd, tp, width = spectra.shape
        vmem = pl.BlockSpec(memory_space=pltpu.VMEM)
        hbm = pl.BlockSpec(memory_space=pl.ANY)
        groups = bw // GROUP
        dma = pltpu.SemaphoreType.DMA
        return pl.pallas_call(
            functools.partial(kernel, n_bands, n_tiles, bw, nd, tp, width),
            out_shape=jax.ShapeDtypeStruct(spectra.shape, F32),
            in_specs=[hbm] + [vmem] * 6,
            out_specs=hbm,
            scratch_shapes=[
                pltpu.VMEM((bw + 4, nd, tp + 16, width), F32),
                pltpu.VMEM((nd, tp, width), F32),
                pltpu.VMEM((bw + 4, nd, tp, width), F32),
                pltpu.VMEM((bw, nd, tp, width), F32),
                pltpu.VMEM((nd, tp, width), F32),
                pltpu.VMEM((tp + 16, width), F32),
                pltpu.VMEM((5, tp, width), F32),
                pltpu.VMEM((4, tp, width), jnp.int32),
                pltpu.VMEM((2, bw * nd, width), F32),
                pltpu.VMEM((2, (bw + 4) * nd, width), F32),
                pltpu.VMEM((tp, width), F32),
                pltpu.VMEM((n_bands, tp, width), F32),
                dma((bw,)), dma((bw,)), dma((2,)), dma((2,)),
                dma((2, groups)), dma((2, groups)),
                dma((2, 2)), dma((2, 2)), dma((n_bands,)), dma((n_bands,)),
            ],
            compiler_params=pltpu.CompilerParams(
                collective_id=0, has_side_effects=True, vmem_limit_bytes=40 * 1024 * 1024
            ),
        )(spectra, sea_mask, neighbors, courant, turning, wind_speed, wind_dir)

    placed = (
        P("bands", None, ("runs", "tiles"), None),
        P("runs", None),
        P(None, ("runs", "tiles"), None),
        P(("runs", "tiles"), None),
        P(("runs", "tiles"), None),
        P(("runs", "tiles"), None),
        P(("runs", "tiles"), None),
    )
    return jax.shard_map(
        per_device,
        mesh=mesh,
        in_specs=placed,
        out_specs=P("bands", None, ("runs", "tiles"), None),
        check_vma=False,
    )
```

```python
import functools
import math

import jax
import jax.numpy as jnp
from jax import lax
from jax.experimental import pallas as pl
from jax.experimental.pallas import tpu as pltpu
from jax.sharding import PartitionSpec as P

MESH = pl.DeviceIdType.MESH
F32 = jnp.float32
LOG2E = 1.0 / math.log(2.0)
GROUP = 2


def lane_gather(x, idx):
    return jnp.take_along_axis(x, idx, axis=1, mode="promise_in_bounds")


def sin_cos(angle):
    y = 0.5 * angle
    z = y * y
    s = 1.0
    for n in (12, 10, 8, 6, 4, 2):
        s = 1.0 - z * s * (1.0 / (n * (n + 1)))
    c = 1.0
    for n in (13, 11, 9, 7, 5, 3, 1):
        c = 1.0 - z * c * (1.0 / (n * (n + 1)))
    s = s * y
    return 2.0 * s * c, 1.0 - 2.0 * s * s


def kernel(
    n_bands, n_tiles, bw, nd, tp, width,
    spectra, mask_in, nbr_in, courant_in, turning_in, wspeed_in, wdir_in, out,
    mask, nbr, courant, turning, wspeed, wdir, ext, e1, e2, obuf, ftab, mext, weights, lanes, hsend, hrecv, macc, mrecv,
    small_sem, load_sem, out_sem, band_send, band_recv, tile_send, tile_recv,
    diag_send, diag_recv, m_send, m_recv,
):
    band = lax.axis_index("bands")
    tile = lax.axis_index("tiles")
    groups = bw // GROUP
    grows = GROUP * nd
    rows = tp + 16
    nf = n_bands * bw
    flat = ext.reshape((bw + 4) * nd * rows, width)
    has_tile = (tile > 0, tile < n_tiles - 1)
    has_band = (band > 0, band < n_bands - 1)
    step = (-1, 1)

    def load(i):
        return pltpu.make_async_copy(
            spectra.at[i], ext.at[i + 2, :, 8 : 8 + tp, :], load_sem.at[i]
        )

    small = [
        pltpu.make_async_copy(source, place, small_sem.at[n])
        for n, (source, place) in enumerate((
            (mask_in, mask), (nbr_in, nbr), (courant_in, courant),
            (turning_in, turning), (wspeed_in, wspeed), (wdir_in, wdir),
        ))
    ]
    for i in range(bw):
        load(i).start()
    for copy in small:
        copy.start()

    barrier = pltpu.get_barrier_semaphore()
    for k in range(1, n_bands):
        pl.semaphore_signal(
            barrier, inc=1, device_id={"bands": lax.rem(band + k, n_bands)}, device_id_type=MESH
        )
    for dt in (1, n_tiles - 1):
        for db in (0, 1, n_bands - 1):
            pl.semaphore_signal(
                barrier, inc=1,
                device_id={
                    "bands": lax.rem(band + db, n_bands), "tiles": lax.rem(tile + dt, n_tiles)
                },
                device_id_type=MESH,
            )
    pl.semaphore_wait(barrier, n_bands - 1 + 6)

    def band_copy(side):
        first, place = (bw - 2, 0) if side == 0 else (0, bw + 2)
        return pltpu.make_async_remote_copy(
            src_ref=spectra.at[first : first + 2],
            dst_ref=ext.at[place : place + 2, :, 8 : 8 + tp, :],
            send_sem=band_send.at[side], recv_sem=band_recv.at[side],
            device_id={"bands": band - step[side]}, device_id_type=MESH,
        )

    def tile_copy(side, g):
        first = pl.multiple_of(g * grows, 8)
        return pltpu.make_async_remote_copy(
            src_ref=hsend.at[side, pl.ds(first, grows), :],
            dst_ref=hrecv.at[side, pl.ds(first + 2 * nd, grows), :],
            send_sem=tile_send.at[side, g], recv_sem=tile_recv.at[side, g],
            device_id={"tiles": tile - step[side]}, device_id_type=MESH,
        )

    def diag_copy(bside, side):
        first, place = ((bw - 2) * nd, 0) if bside == 0 else (0, (bw + 2) * nd)
        return pltpu.make_async_remote_copy(
            src_ref=hsend.at[side, pl.ds(first, 2 * nd), :],
            dst_ref=hrecv.at[side, pl.ds(place, 2 * nd), :],
            send_sem=diag_send.at[bside, side], recv_sem=diag_recv.at[bside, side],
            device_id={"bands": band - step[bside], "tiles": tile - step[side]},
            device_id_type=MESH,
        )

    def m_copy(k):
        return pltpu.make_async_remote_copy(
            src_ref=macc, dst_ref=mrecv.at[k],
            send_sem=m_send.at[k], recv_sem=m_recv.at[k],
            device_id={"bands": lax.rem(band + k, n_bands)}, device_id_type=MESH,
        )

    for side in (0, 1):
        @pl.when(has_band[1 - side])
        def _(side=side):
            band_copy(side).start()

    for g in range(groups):
        for i in range(g * GROUP, (g + 1) * GROUP):
            load(i).wait()
        base = (g * GROUP + 2) * nd * rows
        for side, row in ((0, 8 + tp - 1), (1, 8)):
            hsend[side, pl.ds(g * grows, grows), :] = flat[pl.ds(base + row, grows, stride=rows), :]
            @pl.when(has_tile[1 - side])
            def _(side=side, g=g):
                tile_copy(side, g).start()
    for side in (0, 1):
        for bside in (0, 1):
            @pl.when(has_tile[1 - side] & has_band[1 - bside])
            def _(side=side, bside=bside):
                diag_copy(bside, side).start()

    for copy in small:
        copy.wait()
    first_tile = tile * tp
    below = pl.multiple_of(jnp.maximum(first_tile - 8, 0), 8)
    above = pl.multiple_of(jnp.minimum(first_tile + tp, n_tiles * tp - 8), 8)
    mext[0:8, :] = mask[pl.ds(below, 8), :].astype(F32) * jnp.where(tile > 0, 1.0, 0.0)
    mext[8 : 8 + tp, :] = mask[pl.ds(pl.multiple_of(first_tile, 8), tp), :].astype(F32)
    mext[8 + tp :, :] = mask[pl.ds(above, 8), :].astype(F32) * jnp.where(
        tile < n_tiles - 1, 1.0, 0.0
    )
    for side in (0, 1):
        @pl.when(jnp.logical_not(has_tile[side]))
        def _(side=side):
            hrecv[side] = jnp.zeros(hrecv.shape[1:], F32)
    shifts = (0, 0, -1, 1)
    for h in range(0, tp, 8):
        here = pl.ds(h, 8)
        own = mext[8 + h : 16 + h, :]
        cm = courant[here, :] * own
        for d in range(4):
            link = nbr[d, here, :]
            lane = jnp.bitwise_and(link, width - 1)
            there = lane_gather(mext[8 + h + shifts[d] : 16 + h + shifts[d], :], lane)
            lanes[d, here, :] = lane
            weights[d, here, :] = cm * jnp.where(link < (tp + 2) * width, there, 0.0)
        weights[4, here, :] = cm
        sw, cw = sin_cos(wdir[here, :])
        east, north = wspeed[here, :] * cw, wspeed[here, :] * sw
        for j in range(nd):
            angle = 2.0 * math.pi * (j + 0.5) / nd
            facing = east * math.cos(angle) + north * math.sin(angle)
            ftab[j, here, :] = (0.5 * LOG2E) * jnp.maximum(facing, 0.0)
    macc[...] = jnp.zeros(macc.shape, F32)

    quarter = nd // 4

    def advance(e, summed):
        index = (band * bw + e - 2).astype(F32)
        fraction = index * (1.0 / (nf - 1))
        ratio = jnp.exp(jnp.full((8, width), index, F32) * (-math.log(1.1)))
        for h in range(0, tp, 8):
            here = pl.ds(h, 8)
            own = mext[8 + h : 16 + h, :]
            lane = [lanes[d, here, :] for d in range(4)]
            weight = [weights[d, here, :] * ratio for d in range(4)]
            rcm = weights[4, here, :] * ratio
            total = None
            for k in range(quarter):
                angle = 2.0 * math.pi * (k + 0.5) / nd
                c, s = math.cos(angle), math.sin(angle)
                wx = (weight[0] * c, weight[1] * c)
                wy = (weight[2] * s, weight[3] * s)
                centre = own - rcm * (c + s)
                for j, x, y in (
                    (k, 0, 0), (nd // 2 - 1 - k, 1, 0), (nd // 2 + k, 1, 1), (nd - 1 - k, 0, 1)
                ):
                    mid = ext[e, j, 8 + h : 16 + h, :]
                    off = 8 + h + (1 if y else -1)
                    beside = ext[e, j, off : off + 8, :]
                    value = (
                        centre * mid
                        + wx[x] * lane_gather(mid, lane[x])
                        + wy[y] * lane_gather(beside, lane[2 + y])
                    )
                    e1[j, here, :] = value
                    total = value if total is None else total + value
            if summed:
                macc[here, :] += (0.5 + fraction) * total
            turn = turning[here, :]
            amount = jnp.abs(turn * (0.5 + 0.5 * ratio))
            lower = turn > 0.0
            prev, now = e1[nd - 1, here, :], e1[0, here, :]
            first = now
            for j in range(nd):
                after = e1[j + 1, here, :] if j < nd - 1 else first
                e2[e, j, here, :] = now + amount * (jnp.where(lower, prev, after) - now)
                prev, now = now, after

    def fill_edges(e, count):
        first = pl.multiple_of(e * nd, 4)
        for side, row in ((0, 7), (1, 8 + tp)):
            flat[pl.ds(e * nd * rows + row, count * nd, stride=rows), :] = hrecv[
                side, pl.ds(first, count * nd), :
            ]

    def own_group(g, carry):
        for side in (0, 1):
            @pl.when(has_tile[side])
            def _(side=side):
                tile_copy(side, g).wait_recv()
        fill_edges(2 + g * GROUP, GROUP)

        def one(u, c):
            advance(2 + g * GROUP + u, True)
            return c

        return lax.fori_loop(0, GROUP, one, carry)

    lax.fori_loop(0, groups, own_group, 0)

    for k in range(1, n_bands):
        m_copy(k).start()

    for bside, place in ((0, 0), (1, bw + 2)):
        @pl.when(has_band[bside])
        def _(bside=bside, place=place):
            band_copy(bside).wait_recv()
            for side in (0, 1):
                @pl.when(has_tile[side])
                def _(side=side):
                    diag_copy(bside, side).wait_recv()
            fill_edges(place, 2)

            def one(u, c):
                advance(place + u, False)
                return c

            lax.fori_loop(0, 2, one, 0)

        @pl.when(jnp.logical_not(has_band[bside]))
        def _(place=place):
            e2[place : place + 2] = jnp.zeros((2,) + e2.shape[1:], F32)

    m_sum = macc[...]
    for k in range(1, n_bands):
        m_copy(k).wait()
        m_sum = m_sum + mrecv[k]
    m_sum = m_sum * (1.0 / (nf * nd))
    mrecv[0] = LOG2E * (m_sum / (m_sum + 1.0))

    def store(i):
        return pltpu.make_async_copy(obuf.at[i], out.at[i], out_sem.at[i])

    def finish(i, carry):
        index = (band * bw + i).astype(F32)
        fraction = index * (1.0 / (nf - 1))
        k = 0.05 * (1.0 + fraction)
        for h in range(0, tp, 8):
            here = pl.ds(h, 8)
            damping = (0.2 + fraction) * mrecv[0, here, :]
            for j in range(nd):
                up, down = (j + 3) % nd, (j - 3) % nd
                a1, a2 = e2[i + 4, up, here, :], e2[i + 4, down, here, :]
                b1, b2 = e2[i, down, here, :], e2[i, up, here, :]
                mid = e2[i + 2, j, here, :]
                gain = jnp.exp2(fraction * ftab[j, here, :] - damping)
                inner = mid * ((a1 + b1) + (a2 + b2)) - 2.0 * (a1 * b1 + a2 * b2)
                obuf[i, j, here, :] = mid * (gain + k * inner)
        store(i).start()
        return carry

    lax.fori_loop(0, bw, finish, 0)

    for i in range(bw):
        store(i).wait()
    for side in (0, 1):
        @pl.when(has_band[1 - side])
        def _(side=side):
            band_copy(side).wait_send()

        @pl.when(has_tile[1 - side])
        def _(side=side):
            for g in range(groups):
                tile_copy(side, g).wait_send()

        for bside in (0, 1):
            @pl.when(has_tile[1 - side] & has_band[1 - bside])
            def _(side=side, bside=bside):
                diag_copy(bside, side).wait_send()


def solution(mesh):
    n_bands, n_tiles = mesh.shape["bands"], mesh.shape["tiles"]

    def per_device(spectra, sea_mask, neighbors, courant, turning, wind_speed, wind_dir):
        bw, nd, tp, width = spectra.shape
        hbm = pl.BlockSpec(memory_space=pltpu.HBM)
        groups = bw // GROUP
        dma = pltpu.SemaphoreType.DMA
        return pl.pallas_call(
            functools.partial(kernel, n_bands, n_tiles, bw, nd, tp, width),
            out_shape=jax.ShapeDtypeStruct(spectra.shape, F32),
            in_specs=[hbm] * 7,
            out_specs=hbm,
            scratch_shapes=[
                pltpu.VMEM(sea_mask.shape, jnp.int32),
                pltpu.VMEM(neighbors.shape, jnp.int32),
                pltpu.VMEM((tp, width), F32),
                pltpu.VMEM((tp, width), F32),
                pltpu.VMEM((tp, width), F32),
                pltpu.VMEM((tp, width), F32),
                pltpu.VMEM((bw + 4, nd, tp + 16, width), F32),
                pltpu.VMEM((nd, tp, width), F32),
                pltpu.VMEM((bw + 4, nd, tp, width), F32),
                pltpu.VMEM((bw, nd, tp, width), F32),
                pltpu.VMEM((nd, tp, width), F32),
                pltpu.VMEM((tp + 16, width), F32),
                pltpu.VMEM((5, tp, width), F32),
                pltpu.VMEM((4, tp, width), jnp.int32),
                pltpu.VMEM((2, bw * nd, width), F32),
                pltpu.VMEM((2, (bw + 4) * nd, width), F32),
                pltpu.VMEM((tp, width), F32),
                pltpu.VMEM((n_bands, tp, width), F32),
                dma((6,)), dma((bw,)), dma((bw,)), dma((2,)), dma((2,)),
                dma((2, groups)), dma((2, groups)),
                dma((2, 2)), dma((2, 2)), dma((n_bands,)), dma((n_bands,)),
            ],
            compiler_params=pltpu.CompilerParams(
                collective_id=0, has_side_effects=True, vmem_limit_bytes=40 * 1024 * 1024
            ),
        )(spectra, sea_mask, neighbors, courant, turning, wind_speed, wind_dir)

    placed = (
        P("bands", None, ("runs", "tiles"), None),
        P("runs", None),
        P(None, ("runs", "tiles"), None),
        P(("runs", "tiles"), None),
        P(("runs", "tiles"), None),
        P(("runs", "tiles"), None),
        P(("runs", "tiles"), None),
    )
    return jax.shard_map(
        per_device,
        mesh=mesh,
        in_specs=placed,
        out_specs=P("bands", None, ("runs", "tiles"), None),
        check_vma=False,
    )
```

```python
import functools
import math

import jax
import jax.numpy as jnp
from jax import lax
from jax.experimental import pallas as pl
from jax.experimental.pallas import tpu as pltpu
from jax.sharding import PartitionSpec as P

MESH = pl.DeviceIdType.MESH
F32 = jnp.float32
LOG2E = 1.0 / math.log(2.0)
GROUP = 2


def lane_gather(x, idx):
    return jnp.take_along_axis(x, idx, axis=1, mode="promise_in_bounds")


def sin_cos(angle):
    y = 0.5 * angle
    z = y * y
    s = 1.0
    for n in (12, 10, 8, 6, 4, 2):
        s = 1.0 - z * s * (1.0 / (n * (n + 1)))
    c = 1.0
    for n in (13, 11, 9, 7, 5, 3, 1):
        c = 1.0 - z * c * (1.0 / (n * (n + 1)))
    s = s * y
    return 2.0 * s * c, 1.0 - 2.0 * s * s


def kernel(
    n_bands, n_tiles, bw, nd, tp, width,
    spectra, mask_in, nbr_in, courant_in, turning_in, wspeed_in, wdir_in, out,
    mask, nbr, courant, turning, wspeed, wdir, ext, e1, e2, obuf, ftab, mext, weights, lanes, hsend, hrecv, macc, mrecv,
    small_sem, load_sem, out_sem, band_send, band_recv, tile_send, tile_recv,
    diag_send, diag_recv, m_send, m_recv,
):
    band = lax.axis_index("bands")
    tile = lax.axis_index("tiles")
    groups = bw // GROUP
    grows = GROUP * nd
    rows = tp + 16
    nf = n_bands * bw
    flat = ext.reshape((bw + 4) * nd * rows, width)
    has_tile = (tile > 0, tile < n_tiles - 1)
    has_band = (band > 0, band < n_bands - 1)
    step = (-1, 1)

    def load(i):
        return pltpu.make_async_copy(
            spectra.at[i], ext.at[i + 2, :, 8 : 8 + tp, :], load_sem.at[i]
        )

    small = [
        pltpu.make_async_copy(source, place, small_sem.at[n])
        for n, (source, place) in enumerate((
            (mask_in, mask), (nbr_in, nbr), (courant_in, courant),
            (turning_in, turning), (wspeed_in, wspeed), (wdir_in, wdir),
        ))
    ]
    for i in range(bw):
        load(i).start()
    for copy in small:
        copy.start()

    barrier = pltpu.get_barrier_semaphore()
    for k in range(1, n_bands):
        pl.semaphore_signal(
            barrier, inc=1, device_id={"bands": lax.rem(band + k, n_bands)}, device_id_type=MESH
        )
    for dt in (1, n_tiles - 1):
        for db in (0, 1, n_bands - 1):
            pl.semaphore_signal(
                barrier, inc=1,
                device_id={
                    "bands": lax.rem(band + db, n_bands), "tiles": lax.rem(tile + dt, n_tiles)
                },
                device_id_type=MESH,
            )
    pl.semaphore_wait(barrier, n_bands - 1 + 6)

    def band_copy(side):
        first, place = (bw - 2, 0) if side == 0 else (0, bw + 2)
        return pltpu.make_async_remote_copy(
            src_ref=spectra.at[first : first + 2],
            dst_ref=ext.at[place : place + 2, :, 8 : 8 + tp, :],
            send_sem=band_send.at[side], recv_sem=band_recv.at[side],
            device_id={"bands": band - step[side]}, device_id_type=MESH,
        )

    def tile_copy(side, g):
        first = pl.multiple_of(g * grows, 8)
        return pltpu.make_async_remote_copy(
            src_ref=hsend.at[side, pl.ds(first, grows), :],
            dst_ref=hrecv.at[side, pl.ds(first + 2 * nd, grows), :],
            send_sem=tile_send.at[side, g], recv_sem=tile_recv.at[side, g],
            device_id={"tiles": tile - step[side]}, device_id_type=MESH,
        )

    def diag_copy(bside, side):
        first, place = ((bw - 2) * nd, 0) if bside == 0 else (0, (bw + 2) * nd)
        return pltpu.make_async_remote_copy(
            src_ref=hsend.at[side, pl.ds(first, 2 * nd), :],
            dst_ref=hrecv.at[side, pl.ds(place, 2 * nd), :],
            send_sem=diag_send.at[bside, side], recv_sem=diag_recv.at[bside, side],
            device_id={"bands": band - step[bside], "tiles": tile - step[side]},
            device_id_type=MESH,
        )

    def m_copy(k):
        return pltpu.make_async_remote_copy(
            src_ref=macc, dst_ref=mrecv.at[k],
            send_sem=m_send.at[k], recv_sem=m_recv.at[k],
            device_id={"bands": lax.rem(band + k, n_bands)}, device_id_type=MESH,
        )

    for side in (0, 1):
        @pl.when(has_band[1 - side])
        def _(side=side):
            band_copy(side).start()

    for g in range(groups):
        for i in range(g * GROUP, (g + 1) * GROUP):
            load(i).wait()
        base = (g * GROUP + 2) * nd * rows
        for side, row in ((0, 8 + tp - 1), (1, 8)):
            hsend[side, pl.ds(g * grows, grows), :] = flat[pl.ds(base + row, grows, stride=rows), :]
            @pl.when(has_tile[1 - side])
            def _(side=side, g=g):
                tile_copy(side, g).start()
    for side in (0, 1):
        for bside in (0, 1):
            @pl.when(has_tile[1 - side] & has_band[1 - bside])
            def _(side=side, bside=bside):
                diag_copy(bside, side).start()

    for copy in small:
        copy.wait()
    first_tile = tile * tp
    below = pl.multiple_of(jnp.maximum(first_tile - 8, 0), 8)
    above = pl.multiple_of(jnp.minimum(first_tile + tp, n_tiles * tp - 8), 8)
    mext[0:8, :] = mask[pl.ds(below, 8), :].astype(F32) * jnp.where(tile > 0, 1.0, 0.0)
    mext[8 : 8 + tp, :] = mask[pl.ds(pl.multiple_of(first_tile, 8), tp), :].astype(F32)
    mext[8 + tp :, :] = mask[pl.ds(above, 8), :].astype(F32) * jnp.where(
        tile < n_tiles - 1, 1.0, 0.0
    )
    for side in (0, 1):
        @pl.when(jnp.logical_not(has_tile[side]))
        def _(side=side):
            hrecv[side] = jnp.zeros(hrecv.shape[1:], F32)
    shifts = (0, 0, -1, 1)
    for h in range(0, tp, 8):
        here = pl.ds(h, 8)
        own = mext[8 + h : 16 + h, :]
        cm = courant[here, :] * own
        for d in range(4):
            link = nbr[d, here, :]
            lane = jnp.bitwise_and(link, width - 1)
            there = lane_gather(mext[8 + h + shifts[d] : 16 + h + shifts[d], :], lane)
            lanes[d, here, :] = lane
            weights[d, here, :] = cm * jnp.where(link < (tp + 2) * width, there, 0.0)
        weights[4, here, :] = cm
        sw, cw = sin_cos(wdir[here, :])
        east, north = wspeed[here, :] * cw, wspeed[here, :] * sw
        for j in range(nd):
            angle = 2.0 * math.pi * (j + 0.5) / nd
            facing = east * math.cos(angle) + north * math.sin(angle)
            ftab[j, here, :] = (0.5 * LOG2E) * jnp.maximum(facing, 0.0)
    macc[...] = jnp.zeros(macc.shape, F32)

    quarter = nd // 4

    def advance(e, summed):
        index = (band * bw + e - 2).astype(F32)
        fraction = index * (1.0 / (nf - 1))
        ratio = jnp.exp(jnp.full((8, width), index, F32) * (-math.log(1.1)))
        for h in range(0, tp, 8):
            here = pl.ds(h, 8)
            own = mext[8 + h : 16 + h, :]
            lane = [lanes[d, here, :] for d in range(4)]
            weight = [weights[d, here, :] * ratio for d in range(4)]
            rcm = weights[4, here, :] * ratio
            total = None
            for k in range(quarter):
                angle = 2.0 * math.pi * (k + 0.5) / nd
                c, s = math.cos(angle), math.sin(angle)
                wx = (weight[0] * c, weight[1] * c)
                wy = (weight[2] * s, weight[3] * s)
                centre = own - rcm * (c + s)
                for j, x, y in (
                    (k, 0, 0), (nd // 2 - 1 - k, 1, 0), (nd // 2 + k, 1, 1), (nd - 1 - k, 0, 1)
                ):
                    mid = ext[e, j, 8 + h : 16 + h, :]
                    off = 8 + h + (1 if y else -1)
                    beside = ext[e, j, off : off + 8, :]
                    value = (
                        centre * mid
                        + wx[x] * lane_gather(mid, lane[x])
                        + wy[y] * lane_gather(beside, lane[2 + y])
                    )
                    e1[j, here, :] = value
                    total = value if total is None else total + value
            if summed:
                macc[here, :] += (0.5 + fraction) * total
            turn = turning[here, :]
            amount = jnp.abs(turn * (0.5 + 0.5 * ratio))
            lower = turn > 0.0
            prev, now = e1[nd - 1, here, :], e1[0, here, :]
            first = now
            for j in range(nd):
                after = e1[j + 1, here, :] if j < nd - 1 else first
                e2[e, j, here, :] = now + amount * (jnp.where(lower, prev, after) - now)
                prev, now = now, after

    def fill_edges(e, count):
        first = pl.multiple_of(e * nd, 4)
        for side, row in ((0, 7), (1, 8 + tp)):
            flat[pl.ds(e * nd * rows + row, count * nd, stride=rows), :] = hrecv[
                side, pl.ds(first, count * nd), :
            ]

    def own_group(g, carry):
        for side in (0, 1):
            @pl.when(has_tile[side])
            def _(side=side):
                tile_copy(side, g).wait_recv()
        fill_edges(2 + g * GROUP, GROUP)

        def one(u, c):
            advance(2 + g * GROUP + u, True)
            return c

        return lax.fori_loop(0, GROUP, one, carry)

    lax.fori_loop(0, groups, own_group, 0)

    for k in range(1, n_bands):
        m_copy(k).start()

    for bside, place in ((0, 0), (1, bw + 2)):
        @pl.when(has_band[bside])
        def _(bside=bside, place=place):
            band_copy(bside).wait_recv()
            for side in (0, 1):
                @pl.when(has_tile[side])
                def _(side=side):
                    diag_copy(bside, side).wait_recv()
            fill_edges(place, 2)

            def one(u, c):
                advance(place + u, False)
                return c

            lax.fori_loop(0, 2, one, 0)

        @pl.when(jnp.logical_not(has_band[bside]))
        def _(place=place):
            e2[place : place + 2] = jnp.zeros((2,) + e2.shape[1:], F32)

    m_sum = macc[...]
    for k in range(1, n_bands):
        m_copy(k).wait()
        m_sum = m_sum + mrecv[k]
    m_sum = m_sum * (1.0 / (nf * nd))
    mrecv[0] = LOG2E * (m_sum / (m_sum + 1.0))

    def store(i):
        return pltpu.make_async_copy(obuf.at[i], out.at[i], out_sem.at[i])

    def finish(i, carry):
        index = (band * bw + i).astype(F32)
        fraction = index * (1.0 / (nf - 1))
        k = 0.05 * (1.0 + fraction)
        for h in range(0, tp, 8):
            here = pl.ds(h, 8)
            damping = (0.2 + fraction) * mrecv[0, here, :]
            for j in range(nd):
                up, down = (j + 3) % nd, (j - 3) % nd
                a1, a2 = e2[i + 4, up, here, :], e2[i + 4, down, here, :]
                b1, b2 = e2[i, down, here, :], e2[i, up, here, :]
                mid = e2[i + 2, j, here, :]
                gain = jnp.exp2(fraction * ftab[j, here, :] - damping)
                inner = mid * ((a1 + b1) + (a2 + b2)) - 2.0 * (a1 * b1 + a2 * b2)
                obuf[i, j, here, :] = mid * (gain + k * inner)
        store(i).start()
        return carry

    lax.fori_loop(0, bw, finish, 0)

    for i in range(bw):
        store(i).wait()
    for side in (0, 1):
        @pl.when(has_band[1 - side])
        def _(side=side):
            band_copy(side).wait_send()

        @pl.when(has_tile[1 - side])
        def _(side=side):
            for g in range(groups):
                tile_copy(side, g).wait_send()

        for bside in (0, 1):
            @pl.when(has_tile[1 - side] & has_band[1 - bside])
            def _(side=side, bside=bside):
                diag_copy(bside, side).wait_send()


def solution(mesh):
    n_bands, n_tiles = mesh.shape["bands"], mesh.shape["tiles"]

    def per_device(spectra, sea_mask, neighbors, courant, turning, wind_speed, wind_dir):
        bw, nd, tp, width = spectra.shape
        hbm = pl.BlockSpec(memory_space=pltpu.HBM)
        groups = bw // GROUP
        dma = pltpu.SemaphoreType.DMA
        return pl.pallas_call(
            functools.partial(kernel, n_bands, n_tiles, bw, nd, tp, width),
            out_shape=jax.ShapeDtypeStruct(spectra.shape, F32),
            in_specs=[hbm] * 7,
            out_specs=hbm,
            scratch_shapes=[
                pltpu.VMEM(sea_mask.shape, jnp.int32),
                pltpu.VMEM(neighbors.shape, jnp.int32),
                pltpu.VMEM((tp, width), F32),
                pltpu.VMEM((tp, width), F32),
                pltpu.VMEM((tp, width), F32),
                pltpu.VMEM((tp, width), F32),
                pltpu.VMEM((bw + 4, nd, tp + 16, width), F32),
                pltpu.VMEM((nd, tp, width), F32),
                pltpu.VMEM((bw + 4, nd, tp, width), F32),
                pltpu.VMEM((bw, nd, tp, width), F32),
                pltpu.VMEM((nd, tp, width), F32),
                pltpu.VMEM((tp + 16, width), F32),
                pltpu.VMEM((5, tp, width), F32),
                pltpu.VMEM((4, tp, width), jnp.int32),
                pltpu.VMEM((2, bw * nd, width), F32),
                pltpu.VMEM((2, (bw + 4) * nd, width), F32),
                pltpu.VMEM((tp, width), F32),
                pltpu.VMEM((n_bands, tp, width), F32),
                dma((6,)), dma((bw,)), dma((bw,)), dma((2,)), dma((2,)),
                dma((2, groups)), dma((2, groups)),
                dma((2, 2)), dma((2, 2)), dma((n_bands,)), dma((n_bands,)),
            ],
            compiler_params=pltpu.CompilerParams(
                collective_id=0, has_side_effects=True, vmem_limit_bytes=60 * 1024 * 1024
            ),
        )(spectra, sea_mask, neighbors, courant, turning, wind_speed, wind_dir)

    placed = (
        P("bands", None, ("runs", "tiles"), None),
        P("runs", None),
        P(None, ("runs", "tiles"), None),
        P(("runs", "tiles"), None),
        P(("runs", "tiles"), None),
        P(("runs", "tiles"), None),
        P(("runs", "tiles"), None),
    )
    return jax.shard_map(
        per_device,
        mesh=mesh,
        in_specs=placed,
        out_specs=P("bands", None, ("runs", "tiles"), None),
        check_vma=False,
    )
```

```python
import functools
import math

import jax
import jax.numpy as jnp
from jax import lax
from jax.experimental import pallas as pl
from jax.experimental.pallas import tpu as pltpu
from jax.sharding import PartitionSpec as P

MESH = pl.DeviceIdType.MESH
F32 = jnp.float32
LOG2E = 1.0 / math.log(2.0)
GROUP = 2
PIECES = 1
STEP_VMEM = 56
SOURCE_VMEM = 16


def lane_gather(x, idx):
    return jnp.take_along_axis(x, idx, axis=1, mode="promise_in_bounds")


def sin_cos(angle):
    y = 0.5 * angle
    z = y * y
    s = 1.0
    for n in (12, 10, 8, 6, 4, 2):
        s = 1.0 - z * s * (1.0 / (n * (n + 1)))
    c = 1.0
    for n in (13, 11, 9, 7, 5, 3, 1):
        c = 1.0 - z * c * (1.0 / (n * (n + 1)))
    s = s * y
    return 2.0 * s * c, 1.0 - 2.0 * s * s


def kernel(
    n_bands, n_tiles, bw, nd, tp, width,
    spectra, mask_in, nbr_in, courant_in, turning_in, wspeed_in, wdir_in,
    e2, ftab, gone,
    mask, nbr, courant, turning, wspeed, wdir, ext, e1, mext, weights, lanes, hsend, hrecv, macc, mrecv,
    small_sem, load_sem, band_send, band_recv, tile_send, tile_recv,
    diag_send, diag_recv, m_send, m_recv,
):
    band = lax.axis_index("bands")
    tile = lax.axis_index("tiles")
    groups = bw // GROUP
    grows = GROUP * nd
    rows = tp + 16
    nf = n_bands * bw
    flat = ext.reshape((bw + 4) * nd * rows, width)
    has_tile = (tile > 0, tile < n_tiles - 1)
    has_band = (band > 0, band < n_bands - 1)
    step = (-1, 1)

    def load(i):
        return pltpu.make_async_copy(
            spectra.at[i], ext.at[i + 2, :, 8 : 8 + tp, :], load_sem.at[i]
        )

    small = [
        pltpu.make_async_copy(source, place, small_sem.at[n])
        for n, (source, place) in enumerate((
            (mask_in, mask), (nbr_in, nbr), (courant_in, courant),
            (turning_in, turning), (wspeed_in, wspeed), (wdir_in, wdir),
        ))
    ]
    for i in range(bw):
        load(i).start()
    for copy in small:
        copy.start()

    barrier = pltpu.get_barrier_semaphore()
    for k in range(1, n_bands):
        pl.semaphore_signal(
            barrier, inc=1, device_id={"bands": lax.rem(band + k, n_bands)}, device_id_type=MESH
        )
    count = n_bands - 1
    for side in (0, 1):
        for dest, here in (
            ({}, has_tile[side]),
            ({"bands": band - 1}, has_tile[side] & has_band[0]),
            ({"bands": band + 1}, has_tile[side] & has_band[1]),
        ):
            @pl.when(here)
            def _(side=side, dest=dest):
                pl.semaphore_signal(
                    barrier, inc=1, device_id={"tiles": tile + step[side], **dest},
                    device_id_type=MESH,
                )
            count = count + jnp.where(here, 1, 0)
    pl.semaphore_wait(barrier, count)

    piece = nd // PIECES

    def band_copy(side, n):
        first, place = (bw - 2, 0) if side == 0 else (0, bw + 2)
        u, d = n // PIECES, n % PIECES * piece
        return pltpu.make_async_remote_copy(
            src_ref=spectra.at[first + u, d : d + piece],
            dst_ref=ext.at[place + u, d : d + piece, 8 : 8 + tp, :],
            send_sem=band_send.at[side, n], recv_sem=band_recv.at[side, n],
            device_id={"bands": band - step[side]}, device_id_type=MESH,
        )

    def tile_copy(side, g):
        first = pl.multiple_of(g * grows, 8)
        return pltpu.make_async_remote_copy(
            src_ref=hsend.at[side, pl.ds(first, grows), :],
            dst_ref=hrecv.at[side, pl.ds(first + 2 * nd, grows), :],
            send_sem=tile_send.at[side, g], recv_sem=tile_recv.at[side, g],
            device_id={"tiles": tile - step[side]}, device_id_type=MESH,
        )

    def diag_copy(bside, side):
        first, place = ((bw - 2) * nd, 0) if bside == 0 else (0, (bw + 2) * nd)
        return pltpu.make_async_remote_copy(
            src_ref=hsend.at[side, pl.ds(first, 2 * nd), :],
            dst_ref=hrecv.at[side, pl.ds(place, 2 * nd), :],
            send_sem=diag_send.at[bside, side], recv_sem=diag_recv.at[bside, side],
            device_id={"bands": band - step[bside], "tiles": tile - step[side]},
            device_id_type=MESH,
        )

    def m_copy(k):
        return pltpu.make_async_remote_copy(
            src_ref=macc, dst_ref=mrecv.at[k],
            send_sem=m_send.at[k], recv_sem=m_recv.at[k],
            device_id={"bands": lax.rem(band + k, n_bands)}, device_id_type=MESH,
        )

    for side in (0, 1):
        @pl.when(has_band[1 - side])
        def _(side=side):
            for n in range(2 * PIECES):
                band_copy(side, n).start()

    for g in range(groups):
        for i in range(g * GROUP, (g + 1) * GROUP):
            load(i).wait()
        base = (g * GROUP + 2) * nd * rows
        for side, row in ((0, 8 + tp - 1), (1, 8)):
            hsend[side, pl.ds(g * grows, grows), :] = flat[pl.ds(base + row, grows, stride=rows), :]
            @pl.when(has_tile[1 - side])
            def _(side=side, g=g):
                tile_copy(side, g).start()
    for side in (0, 1):
        for bside in (0, 1):
            @pl.when(has_tile[1 - side] & has_band[1 - bside])
            def _(side=side, bside=bside):
                diag_copy(bside, side).start()

    for copy in small:
        copy.wait()
    first_tile = tile * tp
    below = pl.multiple_of(jnp.maximum(first_tile - 8, 0), 8)
    above = pl.multiple_of(jnp.minimum(first_tile + tp, n_tiles * tp - 8), 8)
    mext[0:8, :] = mask[pl.ds(below, 8), :].astype(F32) * jnp.where(tile > 0, 1.0, 0.0)
    mext[8 : 8 + tp, :] = mask[pl.ds(pl.multiple_of(first_tile, 8), tp), :].astype(F32)
    mext[8 + tp :, :] = mask[pl.ds(above, 8), :].astype(F32) * jnp.where(
        tile < n_tiles - 1, 1.0, 0.0
    )
    for side in (0, 1):
        @pl.when(jnp.logical_not(has_tile[side]))
        def _(side=side):
            hrecv[side] = jnp.zeros(hrecv.shape[1:], F32)
    shifts = (0, 0, -1, 1)
    for h in range(0, tp, 8):
        here = pl.ds(h, 8)
        own = mext[8 + h : 16 + h, :]
        cm = courant[here, :] * own
        for d in range(4):
            link = nbr[d, here, :]
            lane = jnp.bitwise_and(link, width - 1)
            there = lane_gather(mext[8 + h + shifts[d] : 16 + h + shifts[d], :], lane)
            lanes[d, here, :] = lane
            weights[d, here, :] = cm * jnp.where(link < (tp + 2) * width, there, 0.0)
        weights[4, here, :] = cm
        sw, cw = sin_cos(wdir[here, :])
        east, north = wspeed[here, :] * cw, wspeed[here, :] * sw
        for j in range(nd):
            angle = 2.0 * math.pi * (j + 0.5) / nd
            facing = east * math.cos(angle) + north * math.sin(angle)
            ftab[j, here, :] = (0.5 * LOG2E) * jnp.maximum(facing, 0.0)
    macc[...] = jnp.zeros(macc.shape, F32)

    quarter = nd // 4

    def advance(e, summed):
        index = (band * bw + e - 2).astype(F32)
        fraction = index * (1.0 / (nf - 1))
        ratio = jnp.exp(jnp.full((8, width), index, F32) * (-math.log(1.1)))
        for h in range(0, tp, 8):
            here = pl.ds(h, 8)
            own = mext[8 + h : 16 + h, :]
            lane = [lanes[d, here, :] for d in range(4)]
            weight = [weights[d, here, :] * ratio for d in range(4)]
            rcm = weights[4, here, :] * ratio
            total = None
            for k in range(quarter):
                angle = 2.0 * math.pi * (k + 0.5) / nd
                c, s = math.cos(angle), math.sin(angle)
                wx = (weight[0] * c, weight[1] * c)
                wy = (weight[2] * s, weight[3] * s)
                centre = own - rcm * (c + s)
                for j, x, y in (
                    (k, 0, 0), (nd // 2 - 1 - k, 1, 0), (nd // 2 + k, 1, 1), (nd - 1 - k, 0, 1)
                ):
                    mid = ext[e, j, 8 + h : 16 + h, :]
                    off = 8 + h + (1 if y else -1)
                    beside = ext[e, j, off : off + 8, :]
                    value = (
                        centre * mid
                        + wx[x] * lane_gather(mid, lane[x])
                        + wy[y] * lane_gather(beside, lane[2 + y])
                    )
                    e1[j, here, :] = value
                    total = value if total is None else total + value
            if summed:
                macc[here, :] += (0.5 + fraction) * total
            turn = turning[here, :]
            amount = jnp.abs(turn * (0.5 + 0.5 * ratio))
            lower = turn > 0.0
            prev, now = e1[nd - 1, here, :], e1[0, here, :]
            first = now
            for j in range(nd):
                after = e1[j + 1, here, :] if j < nd - 1 else first
                e2[e, j, here, :] = now + amount * (jnp.where(lower, prev, after) - now)
                prev, now = now, after

    def fill_edges(e, count):
        first = pl.multiple_of(e * nd, 4)
        for side, row in ((0, 7), (1, 8 + tp)):
            flat[pl.ds(e * nd * rows + row, count * nd, stride=rows), :] = hrecv[
                side, pl.ds(first, count * nd), :
            ]

    def own_group(g, carry):
        for side in (0, 1):
            @pl.when(has_tile[side])
            def _(side=side):
                tile_copy(side, g).wait_recv()
        fill_edges(2 + g * GROUP, GROUP)

        def one(u, c):
            advance(2 + g * GROUP + u, True)
            return c

        return lax.fori_loop(0, GROUP, one, carry)

    lax.fori_loop(0, groups, own_group, 0)

    for k in range(1, n_bands):
        m_copy(k).start()

    for bside, place in ((0, 0), (1, bw + 2)):
        @pl.when(has_band[bside])
        def _(bside=bside, place=place):
            for n in range(2 * PIECES):
                band_copy(bside, n).wait_recv()
            for side in (0, 1):
                @pl.when(has_tile[side])
                def _(side=side):
                    diag_copy(bside, side).wait_recv()
            fill_edges(place, 2)

            def one(u, c):
                advance(place + u, False)
                return c

            lax.fori_loop(0, 2, one, 0)

        @pl.when(jnp.logical_not(has_band[bside]))
        def _(place=place):
            e2[place : place + 2] = jnp.zeros((2,) + e2.shape[1:], F32)

    m_sum = macc[...]
    for k in range(1, n_bands):
        m_copy(k).wait()
        m_sum = m_sum + mrecv[k]
    m_sum = m_sum * (1.0 / (nf * nd))
    gone[...] = LOG2E * (m_sum / (m_sum + 1.0))

    for side in (0, 1):
        @pl.when(has_band[1 - side])
        def _(side=side):
            for n in range(2 * PIECES):
                band_copy(side, n).wait_send()

        @pl.when(has_tile[1 - side])
        def _(side=side):
            for g in range(groups):
                tile_copy(side, g).wait_send()

        for bside in (0, 1):
            @pl.when(has_tile[1 - side] & has_band[1 - bside])
            def _(side=side, bside=bside):
                diag_copy(bside, side).wait_send()


def source_kernel(n_bands, bw, nd, tp, e2, ftab, gone, out, obuf, out_sem):
    band = lax.axis_index("bands")
    nf = n_bands * bw

    def store(i):
        return pltpu.make_async_copy(obuf.at[i], out.at[i], out_sem.at[i])

    def finish(i, carry):
        index = (band * bw + i).astype(F32)
        fraction = index * (1.0 / (nf - 1))
        k = 0.05 * (1.0 + fraction)
        for h in range(0, tp, 8):
            here = pl.ds(h, 8)
            damping = (0.2 + fraction) * gone[here, :]
            for j in range(nd):
                up, down = (j + 3) % nd, (j - 3) % nd
                a1, a2 = e2[i + 4, up, here, :], e2[i + 4, down, here, :]
                b1, b2 = e2[i, down, here, :], e2[i, up, here, :]
                mid = e2[i + 2, j, here, :]
                gain = jnp.exp2(fraction * ftab[j, here, :] - damping)
                inner = mid * ((a1 + b1) + (a2 + b2)) - 2.0 * (a1 * b1 + a2 * b2)
                obuf[i, j, here, :] = mid * (gain + k * inner)
        store(i).start()
        return carry

    lax.fori_loop(0, bw, finish, 0)

    for i in range(bw):
        store(i).wait()


def solution(mesh):
    n_bands, n_tiles = mesh.shape["bands"], mesh.shape["tiles"]

    def per_device(spectra, sea_mask, neighbors, courant, turning, wind_speed, wind_dir):
        bw, nd, tp, width = spectra.shape
        hbm = pl.BlockSpec(memory_space=pltpu.HBM)
        groups = bw // GROUP
        dma = pltpu.SemaphoreType.DMA
        vmem = pl.BlockSpec(memory_space=pltpu.VMEM)
        stepped = pl.pallas_call(
            functools.partial(kernel, n_bands, n_tiles, bw, nd, tp, width),
            out_shape=[
                pltpu.VMEM((bw + 4, nd, tp, width), F32),
                pltpu.VMEM((nd, tp, width), F32),
                pltpu.VMEM((tp, width), F32),
            ],
            in_specs=[hbm] * 7,
            out_specs=[vmem] * 3,
            scratch_shapes=[
                pltpu.VMEM(sea_mask.shape, jnp.int32),
                pltpu.VMEM(neighbors.shape, jnp.int32),
                pltpu.VMEM((tp, width), F32),
                pltpu.VMEM((tp, width), F32),
                pltpu.VMEM((tp, width), F32),
                pltpu.VMEM((tp, width), F32),
                pltpu.VMEM((bw + 4, nd, tp + 16, width), F32),
                pltpu.VMEM((nd, tp, width), F32),
                pltpu.VMEM((tp + 16, width), F32),
                pltpu.VMEM((5, tp, width), F32),
                pltpu.VMEM((4, tp, width), jnp.int32),
                pltpu.VMEM((2, bw * nd, width), F32),
                pltpu.VMEM((2, (bw + 4) * nd, width), F32),
                pltpu.VMEM((tp, width), F32),
                pltpu.VMEM((n_bands, tp, width), F32),
                dma((6,)), dma((bw,)), dma((2, 2 * PIECES)), dma((2, 2 * PIECES)),
                dma((2, groups)), dma((2, groups)),
                dma((2, 2)), dma((2, 2)), dma((n_bands,)), dma((n_bands,)),
            ],
            compiler_params=pltpu.CompilerParams(
                collective_id=0, has_side_effects=True, vmem_limit_bytes=STEP_VMEM * 1024 * 1024
            ),
        )(spectra, sea_mask, neighbors, courant, turning, wind_speed, wind_dir)
        return pl.pallas_call(
            functools.partial(source_kernel, n_bands, bw, nd, tp),
            out_shape=jax.ShapeDtypeStruct(spectra.shape, F32),
            in_specs=[vmem] * 3,
            out_specs=pl.BlockSpec(memory_space=pl.ANY),
            scratch_shapes=[pltpu.VMEM((bw, nd, tp, width), F32), dma((bw,))],
            compiler_params=pltpu.CompilerParams(vmem_limit_bytes=SOURCE_VMEM * 1024 * 1024),
        )(*stepped)

    placed = (
        P("bands", None, ("runs", "tiles"), None),
        P("runs", None),
        P(None, ("runs", "tiles"), None),
        P(("runs", "tiles"), None),
        P(("runs", "tiles"), None),
        P(("runs", "tiles"), None),
        P(("runs", "tiles"), None),
    )
    return jax.shard_map(
        per_device,
        mesh=mesh,
        in_specs=placed,
        out_specs=P("bands", None, ("runs", "tiles"), None),
        check_vma=False,
    )
```

```python
import functools
import math

import jax
import jax.numpy as jnp
from jax import lax
from jax.experimental import pallas as pl
from jax.experimental.pallas import tpu as pltpu
from jax.sharding import PartitionSpec as P

MESH = pl.DeviceIdType.MESH
F32 = jnp.float32
LOG2E = 1.0 / math.log(2.0)
GROUP = 2
PIECES = 1
STEP_VMEM = 52
SOURCE_VMEM = 16


def lane_gather(x, idx):
    return jnp.take_along_axis(x, idx, axis=1, mode="promise_in_bounds")


def sin_cos(angle):
    y = 0.5 * angle
    z = y * y
    s = 1.0
    for n in (12, 10, 8, 6, 4, 2):
        s = 1.0 - z * s * (1.0 / (n * (n + 1)))
    c = 1.0
    for n in (13, 11, 9, 7, 5, 3, 1):
        c = 1.0 - z * c * (1.0 / (n * (n + 1)))
    s = s * y
    return 2.0 * s * c, 1.0 - 2.0 * s * s


def kernel(
    n_bands, n_tiles, bw, nd, tp, width,
    spectra, mask_in, nbr_in, courant_in, turning_in, wspeed_in, wdir_in,
    e2, ftab, gone, inner,
    mask, nbr, courant, turning, wspeed, wdir, ext, e1, mext, weights, lanes, hsend, hrecv, macc, mrecv,
    small_sem, load_sem, band_send, band_recv, tile_send, tile_recv,
    diag_send, diag_recv, m_send, m_recv,
):
    band = lax.axis_index("bands")
    tile = lax.axis_index("tiles")
    groups = bw // GROUP
    grows = GROUP * nd
    rows = tp + 16
    nf = n_bands * bw
    flat = ext.reshape((bw + 4) * nd * rows, width)
    has_tile = (tile > 0, tile < n_tiles - 1)
    has_band = (band > 0, band < n_bands - 1)
    step = (-1, 1)

    def load(i):
        return pltpu.make_async_copy(
            spectra.at[i], ext.at[i + 2, :, 8 : 8 + tp, :], load_sem.at[i]
        )

    small = [
        pltpu.make_async_copy(source, place, small_sem.at[n])
        for n, (source, place) in enumerate((
            (mask_in, mask), (nbr_in, nbr), (courant_in, courant),
            (turning_in, turning), (wspeed_in, wspeed), (wdir_in, wdir),
        ))
    ]
    for i in range(bw):
        load(i).start()
    for copy in small:
        copy.start()

    barrier = pltpu.get_barrier_semaphore()
    for k in range(1, n_bands):
        pl.semaphore_signal(
            barrier, inc=1, device_id={"bands": lax.rem(band + k, n_bands)}, device_id_type=MESH
        )
    count = n_bands - 1
    for side in (0, 1):
        for dest, here in (
            ({}, has_tile[side]),
            ({"bands": band - 1}, has_tile[side] & has_band[0]),
            ({"bands": band + 1}, has_tile[side] & has_band[1]),
        ):
            @pl.when(here)
            def _(side=side, dest=dest):
                pl.semaphore_signal(
                    barrier, inc=1, device_id={"tiles": tile + step[side], **dest},
                    device_id_type=MESH,
                )
            count = count + jnp.where(here, 1, 0)
    pl.semaphore_wait(barrier, count)

    piece = nd // PIECES

    def band_copy(side, n):
        first, place = (bw - 2, 0) if side == 0 else (0, bw + 2)
        u, d = n // PIECES, n % PIECES * piece
        return pltpu.make_async_remote_copy(
            src_ref=spectra.at[first + u, d : d + piece],
            dst_ref=ext.at[place + u, d : d + piece, 8 : 8 + tp, :],
            send_sem=band_send.at[side, n], recv_sem=band_recv.at[side, n],
            device_id={"bands": band - step[side]}, device_id_type=MESH,
        )

    def tile_copy(side, g):
        first = pl.multiple_of(g * grows, 8)
        return pltpu.make_async_remote_copy(
            src_ref=hsend.at[side, pl.ds(first, grows), :],
            dst_ref=hrecv.at[side, pl.ds(first + 2 * nd, grows), :],
            send_sem=tile_send.at[side, g], recv_sem=tile_recv.at[side, g],
            device_id={"tiles": tile - step[side]}, device_id_type=MESH,
        )

    def diag_copy(bside, side):
        first, place = ((bw - 2) * nd, 0) if bside == 0 else (0, (bw + 2) * nd)
        return pltpu.make_async_remote_copy(
            src_ref=hsend.at[side, pl.ds(first, 2 * nd), :],
            dst_ref=hrecv.at[side, pl.ds(place, 2 * nd), :],
            send_sem=diag_send.at[bside, side], recv_sem=diag_recv.at[bside, side],
            device_id={"bands": band - step[bside], "tiles": tile - step[side]},
            device_id_type=MESH,
        )

    def m_copy(k):
        return pltpu.make_async_remote_copy(
            src_ref=macc, dst_ref=mrecv.at[k],
            send_sem=m_send.at[k], recv_sem=m_recv.at[k],
            device_id={"bands": lax.rem(band + k, n_bands)}, device_id_type=MESH,
        )

    for side in (0, 1):
        @pl.when(has_band[1 - side])
        def _(side=side):
            for n in range(2 * PIECES):
                band_copy(side, n).start()

    for g in range(groups):
        for i in range(g * GROUP, (g + 1) * GROUP):
            load(i).wait()
        base = (g * GROUP + 2) * nd * rows
        for side, row in ((0, 8 + tp - 1), (1, 8)):
            hsend[side, pl.ds(g * grows, grows), :] = flat[pl.ds(base + row, grows, stride=rows), :]
            @pl.when(has_tile[1 - side])
            def _(side=side, g=g):
                tile_copy(side, g).start()
    for side in (0, 1):
        for bside in (0, 1):
            @pl.when(has_tile[1 - side] & has_band[1 - bside])
            def _(side=side, bside=bside):
                diag_copy(bside, side).start()

    for copy in small:
        copy.wait()
    first_tile = tile * tp
    below = pl.multiple_of(jnp.maximum(first_tile - 8, 0), 8)
    above = pl.multiple_of(jnp.minimum(first_tile + tp, n_tiles * tp - 8), 8)
    mext[0:8, :] = mask[pl.ds(below, 8), :].astype(F32) * jnp.where(tile > 0, 1.0, 0.0)
    mext[8 : 8 + tp, :] = mask[pl.ds(pl.multiple_of(first_tile, 8), tp), :].astype(F32)
    mext[8 + tp :, :] = mask[pl.ds(above, 8), :].astype(F32) * jnp.where(
        tile < n_tiles - 1, 1.0, 0.0
    )
    for side in (0, 1):
        @pl.when(jnp.logical_not(has_tile[side]))
        def _(side=side):
            hrecv[side] = jnp.zeros(hrecv.shape[1:], F32)
    shifts = (0, 0, -1, 1)
    for h in range(0, tp, 8):
        here = pl.ds(h, 8)
        own = mext[8 + h : 16 + h, :]
        cm = courant[here, :] * own
        for d in range(4):
            link = nbr[d, here, :]
            lane = jnp.bitwise_and(link, width - 1)
            there = lane_gather(mext[8 + h + shifts[d] : 16 + h + shifts[d], :], lane)
            lanes[d, here, :] = lane
            weights[d, here, :] = cm * jnp.where(link < (tp + 2) * width, there, 0.0)
        weights[4, here, :] = cm
        sw, cw = sin_cos(wdir[here, :])
        east, north = wspeed[here, :] * cw, wspeed[here, :] * sw
        for j in range(nd):
            angle = 2.0 * math.pi * (j + 0.5) / nd
            facing = east * math.cos(angle) + north * math.sin(angle)
            ftab[j, here, :] = (0.5 * LOG2E) * jnp.maximum(facing, 0.0)
    macc[...] = jnp.zeros(macc.shape, F32)

    quarter = nd // 4

    def advance(e, summed):
        index = (band * bw + e - 2).astype(F32)
        fraction = index * (1.0 / (nf - 1))
        ratio = jnp.exp(jnp.full((8, width), index, F32) * (-math.log(1.1)))
        for h in range(0, tp, 8):
            here = pl.ds(h, 8)
            own = mext[8 + h : 16 + h, :]
            lane = [lanes[d, here, :] for d in range(4)]
            weight = [weights[d, here, :] * ratio for d in range(4)]
            rcm = weights[4, here, :] * ratio
            total = None
            for k in range(quarter):
                angle = 2.0 * math.pi * (k + 0.5) / nd
                c, s = math.cos(angle), math.sin(angle)
                wx = (weight[0] * c, weight[1] * c)
                wy = (weight[2] * s, weight[3] * s)
                centre = own - rcm * (c + s)
                for j, x, y in (
                    (k, 0, 0), (nd // 2 - 1 - k, 1, 0), (nd // 2 + k, 1, 1), (nd - 1 - k, 0, 1)
                ):
                    mid = ext[e, j, 8 + h : 16 + h, :]
                    off = 8 + h + (1 if y else -1)
                    beside = ext[e, j, off : off + 8, :]
                    value = (
                        centre * mid
                        + wx[x] * lane_gather(mid, lane[x])
                        + wy[y] * lane_gather(beside, lane[2 + y])
                    )
                    e1[j, here, :] = value
                    total = value if total is None else total + value
            if summed:
                macc[here, :] += (0.5 + fraction) * total
            turn = turning[here, :]
            amount = jnp.abs(turn * (0.5 + 0.5 * ratio))
            lower = turn > 0.0
            prev, now = e1[nd - 1, here, :], e1[0, here, :]
            first = now
            for j in range(nd):
                after = e1[j + 1, here, :] if j < nd - 1 else first
                e2[e, j, here, :] = now + amount * (jnp.where(lower, prev, after) - now)
                prev, now = now, after

    def fill_edges(e, count):
        first = pl.multiple_of(e * nd, 4)
        for side, row in ((0, 7), (1, 8 + tp)):
            flat[pl.ds(e * nd * rows + row, count * nd, stride=rows), :] = hrecv[
                side, pl.ds(first, count * nd), :
            ]

    def own_group(g, carry):
        for side in (0, 1):
            @pl.when(has_tile[side])
            def _(side=side):
                tile_copy(side, g).wait_recv()
        fill_edges(2 + g * GROUP, GROUP)

        def one(u, c):
            advance(2 + g * GROUP + u, True)
            return c

        return lax.fori_loop(0, GROUP, one, carry)

    lax.fori_loop(0, groups, own_group, 0)

    for k in range(1, n_bands):
        m_copy(k).start()

    def interior(i, carry):
        fraction = (band * bw + i).astype(F32) * (1.0 / (nf - 1))
        for h in range(0, tp, 8):
            here = pl.ds(h, 8)
            for j in range(nd):
                inner[i - 2, j, here, :] = transfer(
                    e2, i, j, nd, here, 0.05 * (1.0 + fraction)
                )
        return carry

    lax.fori_loop(2, bw - 2, interior, 0)

    for bside, place in ((0, 0), (1, bw + 2)):
        @pl.when(has_band[bside])
        def _(bside=bside, place=place):
            for n in range(2 * PIECES):
                band_copy(bside, n).wait_recv()
            for side in (0, 1):
                @pl.when(has_tile[side])
                def _(side=side):
                    diag_copy(bside, side).wait_recv()
            fill_edges(place, 2)

            def one(u, c):
                advance(place + u, False)
                return c

            lax.fori_loop(0, 2, one, 0)

        @pl.when(jnp.logical_not(has_band[bside]))
        def _(place=place):
            e2[place : place + 2] = jnp.zeros((2,) + e2.shape[1:], F32)

    m_sum = macc[...]
    for k in range(1, n_bands):
        m_copy(k).wait()
        m_sum = m_sum + mrecv[k]
    m_sum = m_sum * (1.0 / (nf * nd))
    gone[...] = LOG2E * (m_sum / (m_sum + 1.0))

    for side in (0, 1):
        @pl.when(has_band[1 - side])
        def _(side=side):
            for n in range(2 * PIECES):
                band_copy(side, n).wait_send()

        @pl.when(has_tile[1 - side])
        def _(side=side):
            for g in range(groups):
                tile_copy(side, g).wait_send()

        for bside in (0, 1):
            @pl.when(has_tile[1 - side] & has_band[1 - bside])
            def _(side=side, bside=bside):
                diag_copy(bside, side).wait_send()


def transfer(e2, i, j, nd, here, k):
    up, down = (j + 3) % nd, (j - 3) % nd
    a1, a2 = e2[i + 4, up, here, :], e2[i + 4, down, here, :]
    b1, b2 = e2[i, down, here, :], e2[i, up, here, :]
    mid = e2[i + 2, j, here, :]
    return (k * mid) * (mid * ((a1 + b1) + (a2 + b2)) - 2.0 * (a1 * b1 + a2 * b2))


def source_kernel(n_bands, bw, nd, tp, e2, ftab, gone, inner, out, obuf, out_sem):
    band = lax.axis_index("bands")
    nf = n_bands * bw

    def store(i):
        return pltpu.make_async_copy(obuf.at[i], out.at[i], out_sem.at[i])

    def finish(i, ready):
        fraction = (band * bw + i).astype(F32) * (1.0 / (nf - 1))
        k = 0.05 * (1.0 + fraction)
        for h in range(0, tp, 8):
            here = pl.ds(h, 8)
            damping = (0.2 + fraction) * gone[here, :]
            for j in range(nd):
                gain = jnp.exp2(fraction * ftab[j, here, :] - damping)
                if ready:
                    extra = inner[i - 2, j, here, :]
                else:
                    extra = transfer(e2, i, j, nd, here, k)
                obuf[i, j, here, :] = e2[i + 2, j, here, :] * gain + extra
        store(i).start()

    for low, high, ready in ((0, 2, False), (bw - 2, bw, False), (2, bw - 2, True)):
        def one(i, carry, ready=ready):
            finish(i, ready)
            return carry

        lax.fori_loop(low, high, one, 0)

    for i in range(bw):
        store(i).wait()


def solution(mesh):
    n_bands, n_tiles = mesh.shape["bands"], mesh.shape["tiles"]

    def per_device(spectra, sea_mask, neighbors, courant, turning, wind_speed, wind_dir):
        bw, nd, tp, width = spectra.shape
        hbm = pl.BlockSpec(memory_space=pltpu.HBM)
        groups = bw // GROUP
        dma = pltpu.SemaphoreType.DMA
        vmem = pl.BlockSpec(memory_space=pltpu.VMEM)
        stepped = pl.pallas_call(
            functools.partial(kernel, n_bands, n_tiles, bw, nd, tp, width),
            out_shape=[
                pltpu.VMEM((bw + 4, nd, tp, width), F32),
                pltpu.VMEM((nd, tp, width), F32),
                pltpu.VMEM((tp, width), F32),
                pltpu.VMEM((bw - 4, nd, tp, width), F32),
            ],
            in_specs=[hbm] * 7,
            out_specs=[vmem] * 4,
            scratch_shapes=[
                pltpu.VMEM(sea_mask.shape, jnp.int32),
                pltpu.VMEM(neighbors.shape, jnp.int32),
                pltpu.VMEM((tp, width), F32),
                pltpu.VMEM((tp, width), F32),
                pltpu.VMEM((tp, width), F32),
                pltpu.VMEM((tp, width), F32),
                pltpu.VMEM((bw + 4, nd, tp + 16, width), F32),
                pltpu.VMEM((nd, tp, width), F32),
                pltpu.VMEM((tp + 16, width), F32),
                pltpu.VMEM((5, tp, width), F32),
                pltpu.VMEM((4, tp, width), jnp.int32),
                pltpu.VMEM((2, bw * nd, width), F32),
                pltpu.VMEM((2, (bw + 4) * nd, width), F32),
                pltpu.VMEM((tp, width), F32),
                pltpu.VMEM((n_bands, tp, width), F32),
                dma((6,)), dma((bw,)), dma((2, 2 * PIECES)), dma((2, 2 * PIECES)),
                dma((2, groups)), dma((2, groups)),
                dma((2, 2)), dma((2, 2)), dma((n_bands,)), dma((n_bands,)),
            ],
            compiler_params=pltpu.CompilerParams(
                collective_id=0, has_side_effects=True, vmem_limit_bytes=STEP_VMEM * 1024 * 1024
            ),
        )(spectra, sea_mask, neighbors, courant, turning, wind_speed, wind_dir)
        return pl.pallas_call(
            functools.partial(source_kernel, n_bands, bw, nd, tp),
            out_shape=jax.ShapeDtypeStruct(spectra.shape, F32),
            in_specs=[vmem] * 4,
            out_specs=pl.BlockSpec(memory_space=pl.ANY),
            scratch_shapes=[pltpu.VMEM((bw, nd, tp, width), F32), dma((bw,))],
            compiler_params=pltpu.CompilerParams(vmem_limit_bytes=SOURCE_VMEM * 1024 * 1024),
        )(*stepped)

    placed = (
        P("bands", None, ("runs", "tiles"), None),
        P("runs", None),
        P(None, ("runs", "tiles"), None),
        P(("runs", "tiles"), None),
        P(("runs", "tiles"), None),
        P(("runs", "tiles"), None),
        P(("runs", "tiles"), None),
    )
    return jax.shard_map(
        per_device,
        mesh=mesh,
        in_specs=placed,
        out_specs=P("bands", None, ("runs", "tiles"), None),
        check_vma=False,
    )
```
